32 devices in a mesh: frame: 16 (over z, y, core), fsdp: 2 (over x).
Axes of the slice: x: 2, y: 2, z: 4, core: 2. Of those that a mesh axis runs over, the one named last changes fastest.
Arguments:
- frames: bfloat16 [2, 2, 16, 128, 1280], P('fsdp', None, 'frame'), may hold values from -6 to 6
- cotangent: bfloat16 [2, 2, 16, 128, 1280], P('fsdp', None, 'frame'), may hold values from -6 to 6
- block_lengths: int32 [2, 2, 1], P('fsdp'), may hold values from 1 to 16, as said below
- qkv_weight: bfloat16 [3, 1280, 1280], P(None, 'fsdp'), may hold values from -0.15625 to 0.15625
- pair_weight: bfloat16 [2, 1280, 1280], P(None, 'fsdp'), may hold values from -0.15625 to 0.15625
- attn_out_weight: bfloat16 [1280, 1280], P('fsdp'), may hold values from -0.3125 to 0.3125
- ff_up_weight: bfloat16 [1280, 5120], P('fsdp'), may hold values from -0.15625 to 0.15625
- ff_down_weight: bfloat16 [5120, 1280], P('fsdp'), may hold values from -0.15625 to 0.15625
- norm_gains: float32 [3, 1280], replicated, may hold values from 0.1 to 1.9
- biases: float32 [7, 1280], replicated, may hold values from -3 to 3
- up_bias: float32 [5120], replicated, may hold values from -3 to 3
Outputs:
- result: bfloat16 [2, 2, 16, 128, 1280], P('fsdp', None, 'frame')
- frames_grad: bfloat16 [2, 2, 16, 128, 1280], P('fsdp', None, 'frame')
- qkv_grad: float32 [3, 1280, 1280], P(None, 'fsdp', 'frame')
- pair_grad: float32 [2, 1280, 1280], P(None, 'fsdp', 'frame')
- attn_out_grad: float32 [1280, 1280], P('fsdp', 'frame')
- ff_up_grad: float32 [1280, 5120], P('fsdp', 'frame')
- ff_down_grad: float32 [5120, 1280], P('fsdp', 'frame')
- gains_grad: float32 [3, 1280], replicated
- biases_grad: float32 [7, 1280], replicated
- up_bias_grad: float32 [5120], replicated
The draws below stay inside these ranges and needn't reach their ends.
Inputs may be any that keep to these rules, and one draw needn't show every extreme that they name: `block_lengths`: block b of a micro-batch holds frames b * 16 to b * 16 + 15: one clip of 16 frames where its length is 16, 16 single images of length 1 where it is 1; no other lengths occur.
All inputs are finite; a program needn't handle non-finite values.
Results may differ from the reference program's by a relative error of at most 0.015.
Values may be sent and summed in bfloat16 or wider, within the bound.
No kernel may reach another device: no remote copies, remote signals or barrier semaphores. Data moves between devices by JAX's collectives and lax.ppermute only.
A program may use at most 384 MiB of HBM per device.

```python
import math
import jax
import jax.numpy as jnp
from jax import lax

C = 1280
FF = 5120
HEADS = 8
GROUPS = 32
HW = 128
CLIP = 16
MB = 2
FRAMES = 16
BLOCKS = 1
DATA = 2


def draw_block_lengths(key, part):
    picks = jax.random.randint(key, (DATA, MB, BLOCKS), 0, 4)
    lengths = jnp.where(picks < 3, CLIP, 1).astype(jnp.int32)
    lengths = lengths.at[0, 0, 0].set(CLIP)
    lengths = lengths.at[DATA - 1, MB - 1, BLOCKS - 1].set(1)
    return lengths


def raised(values, rng, source, target, blocks, factor):
    def block_of(dim):
        return (jnp.arange(values.shape[dim]) // (values.shape[dim] // blocks)).reshape((-1,) + (1,) * (values.ndim - 1 - dim))

    one_side = jax.random.permutation(rng, blocks)[block_of(target)]
    far = (block_of(target) + blocks // 2) % blocks
    return jnp.where((block_of(source) == one_side) | (block_of(source) == far), factor * values, values)


def shard_levels(own_key, extent, split, low, largest):
    def one(axis_at, blocks):
        heights = jax.random.uniform(jax.random.fold_in(jax.random.fold_in(own_key, 6), axis_at), (blocks,), jnp.float32, low / len(split), largest / len(split))
        return jnp.repeat(jnp.exp(heights), extent[axis_at] // blocks).reshape((-1,) + (1,) * (len(extent) - axis_at - 1))

    gain = one(*split[0])
    for cut in split[1:]:
        gain = gain * one(*cut)
    return gain


def centred(key, dims, deviation, bound, cuts=(), held_as=jnp.bfloat16):
    values = deviation * jax.random.normal(key, dims, jnp.float32)
    if cuts:
        values = values * shard_levels(key, dims, cuts, -0.22, 0.18)
    return jnp.clip(values, -bound, bound).astype(held_as)


def gaussian_with(rng, dims, width, bound, cuts, heavy, held_as=jnp.bfloat16):
    entries = width * jax.random.normal(rng, dims, jnp.float32)
    if cuts:
        entries = entries * shard_levels(rng, dims, cuts, -0.22, 0.18)
    return jnp.clip(raised(entries, jax.random.fold_in(rng, 3), *heavy), -bound, bound).astype(held_as)


def setup_inputs(seed: int = 0) -> dict:
    key_list = jax.random.split(jax.random.key(seed), 12)
    frames = centred(key_list[0], (DATA, MB, FRAMES, HW, C), 1.0, 6.0, ((0, 2), (2, 16)))
    cotangent = gaussian_with(key_list[1], (DATA, MB, FRAMES, HW, C), 1.0, 6.0, ((0, 2), (2, 16)), (2, 4, 16, 2.0))
    block_lengths = draw_block_lengths(jax.random.fold_in(key_list[11], 71), 0)
    qkv_weight = centred(key_list[3], (3, C, C), C ** -0.5, 0.15625, ((1, 2),))
    pair_weight = centred(key_list[4], (2, C, C), C ** -0.5, 0.15625, ((1, 2),))
    attn_out_weight = centred(key_list[5], (C, C), (C // 4) ** -0.5, 0.3125, ((0, 2),))
    ff_up_weight = centred(key_list[6], (C, FF), C ** -0.5, 0.15625, ((0, 2),))
    ff_down_weight = centred(key_list[7], (FF, C), (FF // 4) ** -0.5, 0.15625, ((0, 2),))
    norm_gains = jnp.clip(1.0 + 0.18 * jax.random.normal(key_list[8], (3, C), jnp.float32), 0.1, 1.9)
    biases = centred(key_list[9], (7, C), 0.5, 3.0, (), jnp.float32)
    up_bias = centred(key_list[10], (FF,), 0.5, 3.0, (), jnp.float32)
    return dict(frames=frames, cotangent=cotangent, block_lengths=block_lengths, qkv_weight=qkv_weight, pair_weight=pair_weight, attn_out_weight=attn_out_weight, ff_up_weight=ff_up_weight, ff_down_weight=ff_down_weight, norm_gains=norm_gains, biases=biases, up_bias=up_bias)


@jax.custom_vjp
def low(v):
    return lax.optimization_barrier(v.astype(jnp.bfloat16)).astype(jnp.float32)

@jax.custom_vjp
def low_back(v):
    return v

def low_keep(v):
    return (low(v), None)

def low_pass(kept, grad):
    return (grad,)

def back_keep(v):
    return (v, None)

def back_low(kept, grad):
    return (low(grad),)
low.defvjp(low_keep, low_pass)
low_back.defvjp(back_keep, back_low)

def matmul(matrix, weight):
    return jnp.einsum('fpc,cd->fpd', matrix, weight, precision=lax.Precision.HIGHEST)

def pos_table(block_count):
    steps_col = jnp.arange(CLIP, dtype=jnp.float32)[:, None]
    freq_rates = jnp.exp(jnp.arange(0, C, 2, dtype=jnp.float32) * (-math.log(10000.0) / C))
    angles = steps_col * freq_rates[None, :]
    single = jnp.stack([jnp.sin(angles), jnp.cos(angles)], axis=-1).reshape(CLIP, C)
    return jnp.tile(single, (block_count, 1))[:, None, :]

def layer_norm(values):
    row_mean = lax.optimization_barrier(jnp.mean(values, axis=-1, keepdims=True))
    row_var = lax.optimization_barrier(jnp.mean(jnp.square(values - row_mean), axis=-1, keepdims=True))
    return (values - row_mean) * lax.rsqrt(row_var + 1e-05)

def one_unit(frame_vals, length_row, qkv_weight, pair_weight, attn_out_weight, ff_up_weight, ff_down_weight, norm_gains, biases, up_bias):
    group_width = C // GROUPS
    frame_count = BLOCKS * CLIP
    is_clip = length_row > 1
    clip_mask = jnp.repeat(is_clip.astype(jnp.float32), CLIP)
    grouped = frame_vals.reshape(frame_count, HW, GROUPS, group_width)
    group_mean = lax.optimization_barrier(jnp.mean(grouped, axis=(1, 3), keepdims=True))
    group_var = lax.optimization_barrier(jnp.mean(jnp.square(grouped - group_mean), axis=(1, 3), keepdims=True))
    group_hat = ((grouped - group_mean) * lax.rsqrt(group_var + 1e-06)).reshape(frame_count, HW, C)
    hidden = low(group_hat * norm_gains[0] + biases[0])
    first_res = low_back(low(matmul(hidden, pair_weight[0]) + biases[2]))
    row_hat = layer_norm(first_res)
    inputs = low(row_hat * norm_gains[1] + biases[1] + pos_table(BLOCKS))
    head_shape = (BLOCKS, CLIP, HW, HEADS, C // HEADS)
    queries = low_back(low(matmul(inputs, qkv_weight[0]))).reshape(head_shape)
    key_rows = low_back(low(matmul(inputs, qkv_weight[1]))).reshape(head_shape)
    values = low_back(low(matmul(inputs, qkv_weight[2]))).reshape(head_shape)
    score_scale = (C // HEADS) ** (-0.5)
    scores = jnp.einsum('bqphd,bkphd->bphqk', queries, key_rows, precision=lax.Precision.HIGHEST) * score_scale
    scores = low_back(scores)
    diagonal = jnp.arange(CLIP)[:, None] == jnp.arange(CLIP)[None, :]
    allowed = jnp.logical_or(is_clip[:, None, None, None, None], diagonal)
    scores = jnp.where(allowed, scores, -1000000000.0)
    row_top = lax.optimization_barrier(jnp.max(scores, axis=-1, keepdims=True))
    exp_scores = jnp.exp(scores - row_top)
    prob_float = exp_scores / lax.optimization_barrier(jnp.sum(exp_scores, axis=-1, keepdims=True))
    prob_low = low(prob_float)
    mixed = jnp.einsum('bphqk,bkphd->bqphd', prob_low, values, precision=lax.Precision.HIGHEST)
    mixed = low_back(low(mixed.reshape(frame_count, HW, C)))
    attended = low_back(matmul(mixed, attn_out_weight) + biases[3])
    second_res = low_back(low(first_res + attended))
    ff_hat = layer_norm(second_res)
    ff_in = low(ff_hat * norm_gains[2] + biases[5])
    up = low_back(matmul(ff_in, ff_up_weight) + up_bias)
    act = low(jax.nn.gelu(up, approximate=False))
    ff_out = matmul(act, ff_down_weight) + biases[6]
    third_res = low_back(low(second_res + ff_out))
    branch = low_back(matmul(third_res, pair_weight[1]) + biases[4])
    return frame_vals + clip_mask[:, None, None] * branch

def reference(frames, cotangent, block_lengths, qkv_weight, pair_weight, attn_out_weight, ff_up_weight, ff_down_weight, norm_gains, biases, up_bias):
    unit_count = DATA * MB
    frame_vals = frames.astype(jnp.float32).reshape(unit_count, BLOCKS * CLIP, HW, C)
    length_rows = block_lengths.reshape(unit_count, BLOCKS)

    def forward(frame_all, qkv_all, pair_all, attn_all, up_all, down_all, gain_all, bias_all, upb_all):

        def per_unit(pieces):
            return one_unit(pieces[0], pieces[1], qkv_all, pair_all, attn_all, up_all, down_all, gain_all, bias_all, upb_all)
        return lax.map(jax.checkpoint(per_unit), (frame_all, length_rows))
    outputs, pullback = jax.vjp(forward, frame_vals, qkv_weight.astype(jnp.float32), pair_weight.astype(jnp.float32), attn_out_weight.astype(jnp.float32), ff_up_weight.astype(jnp.float32), ff_down_weight.astype(jnp.float32), norm_gains, biases, up_bias)
    gradients = pullback(cotangent.astype(jnp.float32).reshape(frame_vals.shape))
    return (outputs.reshape(frames.shape).astype(jnp.bfloat16), gradients[0].reshape(frames.shape).astype(jnp.bfloat16), gradients[1], gradients[2], gradients[3], gradients[4], gradients[5], gradients[6], gradients[7], gradients[8])
```

```python
import math

import jax
import jax.numpy as jnp
import numpy as np
from jax import lax
from jax.experimental import pallas as pl
from jax.experimental.pallas import tpu as pltpu
from jax.sharding import PartitionSpec as P

HEADS = 8
GROUPS = 32
CLIP = 16
CORES = 2
BF = jnp.bfloat16
F32 = jnp.float32
HIGH = lax.Precision.HIGHEST
STEP = 64
WIDE = 640


def pos_table(channels):
    steps_col = np.arange(CLIP, dtype=np.float32)[:, None]
    freq_rates = np.exp(
        np.arange(0, channels, 2, dtype=np.float32) * np.float32(-math.log(10000.0) / channels)
    )
    angles = steps_col * freq_rates[None, :]
    return np.stack([np.sin(angles), np.cos(angles)], axis=-1).reshape(CLIP, channels)


def after(value, *deps):
    return lax.optimization_barrier((value,) + deps)[0]


class Grid:
    def __init__(self, channels):
        self.nx = lax.axis_size("fsdp")
        self.nf = lax.axis_size("frame")
        chips = self.nf // CORES
        self.ny = self.nx if chips % self.nx == 0 else 1
        self.nz = chips // self.ny
        at = lax.axis_index("frame")
        self.x = lax.axis_index("fsdp")
        self.c = at % CORES
        self.y = (at // CORES) % self.ny
        z = at // (CORES * self.ny)
        self.n0 = 2 if self.nz % 2 == 0 else 1
        self.z0, self.z1 = z % self.n0, z // self.n0

        rows = channels // self.nx
        self.cores = CORES if rows % (self.ny * CORES * 16) == 0 else 1
        self.block = rows // (self.ny * self.cores)
        self.cell = self.y * self.cores + (self.c if self.cores > 1 else 0)

    def cut(self, shard, index, count, kind):
        rows, cols = shard.shape
        if kind == "tall":
            at = (self.cell * count + index) * self.block
            return lax.dynamic_slice_in_dim(shard, at, self.block, axis=0)
        width = cols // count
        part = lax.slice_in_dim(shard, index * width, (index + 1) * width, axis=1)
        return lax.dynamic_slice_in_dim(part, self.cell * self.block, self.block, axis=0)

    def size(self, axis):
        sizes = {"x": self.nx, "y": self.ny, "c": CORES, "z0": self.n0, "z1": self.nz // self.n0}
        return sizes[axis]

    def at(self, axis):
        return {"x": self.x, "y": self.y, "c": self.c, "z0": self.z0, "z1": self.z1}[axis]

    def shift(self, value, axis, off):
        size = self.size(axis)
        if axis == "x":
            return lax.ppermute(value, "fsdp", [(i, (i + off) % size) for i in range(size)])
        plane = CORES * self.ny
        step = {"c": 1, "y": CORES, "z0": plane, "z1": plane * self.n0}[axis]
        pairs = []
        for i in range(self.nf):
            place = (i // step) % size
            pairs.append((i, i + ((place + off) % size - place) * step))
        return lax.ppermute(value, "frame", pairs)

    def total(self, value):
        bit = 1
        while bit < self.nf:
            value = value + lax.ppermute(value, "frame", [(i, i ^ bit) for i in range(self.nf)])
            bit *= 2
        bit = 1
        while bit < self.nx:
            value = value + lax.ppermute(value, "fsdp", [(i, i ^ bit) for i in range(self.nx)])
            bit *= 2
        return value


class Packet:
    def __init__(self, grid, blocks, *deps):
        self.piece = jnp.stack(blocks)
        if deps:
            self.piece = after(self.piece, *deps)
        self.grid = grid

    def over_x(self):
        grid = self.grid
        self.got = {off: grid.shift(self.piece, "x", off) for off in range(1, grid.nx)}
        return list(self.got.values())

    def over_y(self, deps=(), late=()):
        grid = self.grid
        self.parts, self.mark = {}, []
        for off_x, got in self.got.items():
            got = after(got, *deps) if deps else got
            for off_y in range(grid.ny):
                over_y = grid.shift(got, "y", off_y) if off_y else got
                if off_y and late:
                    over_y = after(over_y, *late)
                for off_c in range(grid.cores):
                    over_c = grid.shift(over_y, "c", off_c) if off_c else over_y
                    self.parts[off_x, off_y, off_c] = over_c
                    if (off_y > 0) + (off_c > 0) == 1:
                        self.mark.append(over_c)
        return self.mark


class Weight:
    def __init__(self, grid, own, lead, blocks, kind):
        self.own, self.lead, self.blocks, self.kind = own, lead, blocks, kind
        self.nx, self.ny, self.cores = grid.nx, grid.ny, grid.cores
        self.rows, self.block = own.shape[1], grid.block
        self.chunks = len(blocks) if kind == "wide" else 1

    @property
    def arrays(self):
        out = [self.own]
        for packet, _ in self.blocks:
            out += list(packet.parts.values())
        return out

    def count(self):
        own = self.chunks
        return own + sum(len(packet.parts) for packet, _ in self.blocks)

    def copies(self, place, find, dst, sems, base):
        x, y, c = place[0], place[1], place[2]
        out, sem = [], base
        width = dst.shape[1] // self.chunks
        for chunk in range(self.chunks):
            cols = pl.ds(chunk * width, width)
            row = pl.multiple_of(x * self.rows, 16)
            target = dst.at[pl.ds(row, self.rows), cols]
            source = find(self.own).at[self.lead, :, cols]
            out.append([pltpu.make_async_copy(source, target, sems.at[sem])])
            sem += 1
        for at, (packet, index) in enumerate(self.blocks):
            chunk = at if self.kind == "wide" else 0
            cols = pl.ds(chunk * width, width)
            for (off_x, off_y, off_c), part in packet.parts.items():
                row = lax.rem(x + self.nx - off_x, self.nx) * self.rows
                cell = lax.rem(y + self.ny - off_y, self.ny) * self.cores
                if self.cores > 1:
                    cell = cell + lax.rem(c + CORES - off_c, CORES)
                if self.kind == "tall":
                    row = row + (cell * len(self.blocks) + at) * self.block
                else:
                    row = row + cell * self.block
                target = dst.at[pl.ds(pl.multiple_of(row, 16), self.block), cols]
                out[chunk].append(
                    pltpu.make_async_copy(find(part).at[index], target, sems.at[sem])
                )
                sem += 1
        return out


def start(copies):
    for copy in copies:
        copy.start()
    return copies


def wait(copies):
    for copy in copies:
        copy.wait()


def run(body, place, dense, weights, outs, scratch, cost):
    vmem = pl.BlockSpec(memory_space=pltpu.VMEM)
    far = {}
    for weight in weights:
        for array in weight.arrays:
            far.setdefault(id(array), array)
    order = list(far)
    count = sum(w.count() for w in weights)

    def kernel(place_ref, *refs):
        inputs, refs = refs[: len(dense)], refs[len(dense) :]
        find, refs = refs[: len(order)], refs[len(order) :]
        out_refs, scratch_refs = refs[: len(outs)], refs[len(outs) :]
        sems, base, groups = scratch_refs[-1], 0, []
        for weight, dst in zip(weights, scratch_refs):
            groups.append(
                weight.copies(place_ref, lambda a: find[order.index(id(a))], dst, sems, base)
            )
            base += weight.count()
        for group in groups:
            for copies in group:
                start(copies)
        body(inputs, groups, out_refs, scratch_refs[:-1])

    return pl.pallas_call(
        kernel,
        out_shape=[jax.ShapeDtypeStruct(shape, dtype) for shape, dtype in outs],
        in_specs=[pl.BlockSpec(memory_space=pltpu.SMEM)]
        + [vmem] * len(dense)
        + [pl.BlockSpec(memory_space=pl.ANY)] * len(order),
        out_specs=[vmem] * len(outs),
        scratch_shapes=[pltpu.VMEM(shape, dtype) for shape, dtype in scratch]
        + [pltpu.SemaphoreType.DMA((count,))],
        compiler_params=pltpu.CompilerParams(vmem_limit_bytes=60 * 2**20),
        cost_estimate=pl.CostEstimate(flops=cost * 10**9, bytes_accessed=0, transcendentals=0),
    )(place, *dense, *far.values())


def dot(left, right):
    return jnp.dot(left, right, preferred_element_type=F32)


def dot_t(left, right):
    return lax.dot_general(left, right, (((1,), (1,)), ((), ())), preferred_element_type=F32)


def dot_0(left, right):
    return lax.dot_general(left, right, (((0,), (0,)), ((), ())), preferred_element_type=F32)


def norm(values):
    cent = values - jnp.mean(values, axis=-1, keepdims=True)
    rstd = lax.rsqrt(jnp.mean(cent * cent, axis=-1, keepdims=True) + 1e-05)
    return cent * rstd, rstd


def norm_back(scaled, hat, rstd):
    return rstd * (
        scaled
        - jnp.mean(scaled, axis=-1, keepdims=True)
        - hat * jnp.mean(scaled * hat, axis=-1, keepdims=True)
    )


def fold(value):
    return jnp.sum(value.reshape(value.shape[0] // 8, 8, value.shape[1]), axis=0)


def members(channels):
    width = channels // GROUPS
    col = lax.broadcasted_iota(jnp.int32, (channels, 128), 0)
    low = lax.broadcasted_iota(jnp.int32, (channels, 128), 1) * width
    return jnp.where((col >= low) & (col < low + width), 1.0, 0.0).astype(F32)


def group_mean(partial, member, count):
    sums = jnp.broadcast_to(jnp.sum(partial, axis=0, keepdims=True), partial.shape)
    inside = jnp.dot(sums, member, precision=HIGH, preferred_element_type=F32) / count
    spread = lax.dot_general(
        inside, member, (((1,), (1,)), ((), ())), precision=HIGH, preferred_element_type=F32
    )
    return spread[:1]


def group_stats(frames, unit, pixels, member):
    channels = frames.shape[1]
    count = float(pixels * (channels // GROUPS))
    chunks = [pl.ds(unit * pixels + at, STEP) for at in range(0, pixels, STEP)]
    mean = group_mean(sum(fold(frames[rows, :].astype(F32)) for rows in chunks), member, count)
    squares = [fold(jnp.square(frames[rows, :].astype(F32) - mean)) for rows in chunks]
    rstd = lax.rsqrt(group_mean(sum(squares), member, count) + 1e-06)
    return chunks, mean, rstd, count


def enter(place, frames, gains, biases, pair0, pixels):
    tokens, channels = frames.shape

    def body(inputs, groups, outs, scratch):
        frames, gains, biases = inputs
        hidden, first = outs
        (weight,) = scratch
        member = members(channels)
        for unit in range(tokens // pixels):
            chunks, mean, rstd, _ = group_stats(frames, unit, pixels, member)
            for rows in chunks:
                hat = (frames[rows, :].astype(F32) - mean) * rstd
                hidden[rows, :] = (hat * gains[0:1, :] + biases[0:1, :]).astype(BF)
        wait(groups[0][0])
        for at in range(0, channels, WIDE):
            cols = pl.ds(at, WIDE)
            first[:, cols] = (dot(hidden[...], weight[:, cols]) + biases[2:3, cols]).astype(BF)

    square = ((tokens, channels), BF)
    return run(
        body, place, [frames, gains, biases], [pair0], [square, square],
        [((channels, channels), BF)], 7,
    )


def project(place, res, gains, biases, positions, qkv):
    tokens, channels = res.shape

    def body(inputs, groups, outs, scratch):
        res, gains, biases, positions = inputs
        rows_in = outs[0]
        for at in range(0, tokens, STEP):
            rows = pl.ds(at, STEP)
            hat, _ = norm(res[rows, :].astype(F32))
            rows_in[rows, :] = (
                hat * gains[1:2, :] + biases[1:2, :] + positions[rows, :]
            ).astype(BF)
        for k in range(3):
            wait(groups[k][0])
            for at in range(0, channels, WIDE):
                cols = pl.ds(at, WIDE)
                outs[1 + k][:, cols] = dot(rows_in[...], scratch[k][:, cols]).astype(BF)

    square = ((tokens, channels), BF)
    return run(
        body, place, [res, gains, biases, positions], qkv, [square] * 4,
        [((channels, channels), BF)] * 3, 8,
    )


def softmax(query, key, seq_col, seq_row, clip_col, scale):
    tokens = query.shape[0]
    scores = dot_t(query, key) * scale
    row = lax.broadcasted_iota(jnp.int32, (tokens, tokens), 0)
    col = lax.broadcasted_iota(jnp.int32, (tokens, tokens), 1)
    scores = jnp.where((clip_col > 0.5) | (row == col), scores, -1000000000.0)
    scores = jnp.where(seq_col == seq_row, scores, -3.0e38)
    powers = jnp.exp(scores - jnp.max(scores, axis=-1, keepdims=True))
    return powers / jnp.sum(powers, axis=-1, keepdims=True)


def attend(place, res, query, key, value, seqs, biases, attn):
    tokens, channels = res.shape
    dim = channels // HEADS

    def body(inputs, groups, outs, scratch):
        res, query, key, value, seq_col, seq_row, clip_col, biases = inputs
        mixed, second = outs
        (weight,) = scratch
        for head in range(HEADS):
            cols = slice(head * dim, head * dim + dim)
            probs = softmax(
                query[:, cols], key[:, cols], seq_col[...], seq_row[...], clip_col[...], dim**-0.5
            )
            mixed[:, cols] = dot(probs.astype(BF), value[:, cols]).astype(BF)
        wait(groups[0][0])
        for at in range(0, channels, WIDE):
            cols = pl.ds(at, WIDE)
            attended = dot(mixed[...], weight[:, cols]) + biases[3:4, cols]
            second[:, cols] = (res[:, cols].astype(F32) + attended).astype(BF)

    square = ((tokens, channels), BF)
    return run(
        body, place, [res, query, key, value, *seqs, biases], [attn], [square, square],
        [((channels, channels), BF)], 12,
    )


def ff_up(place, second, gains, biases, up_bias, up):
    tokens, channels = second.shape
    width = up_bias.shape[1]
    share = width // up.chunks

    def body(inputs, groups, outs, scratch):
        second, gains, biases, up_bias = inputs
        ff_in, act, slope = outs
        (weight,) = scratch
        for at in range(0, tokens, STEP):
            rows = pl.ds(at, STEP)
            hat, _ = norm(second[rows, :].astype(F32))
            ff_in[rows, :] = (hat * gains[2:3, :] + biases[5:6, :]).astype(BF)
        for k in range(up.chunks):
            wait(groups[0][k])

            @pl.loop(0, share // WIDE)
            def _(i):
                cols = pl.ds(pl.multiple_of(k * share + i * WIDE, 128), WIDE)
                upper = dot(ff_in[...], weight[:, cols]) + up_bias[:, cols]
                cdf = 0.5 * (1.0 + lax.erf(upper * (1.0 / math.sqrt(2.0))))
                pdf = jnp.exp(-0.5 * upper * upper) * (1.0 / math.sqrt(2.0 * math.pi))
                act[:, cols] = (upper * cdf).astype(BF)
                slope[:, cols] = cdf + upper * pdf

    return run(
        body, place, [second, gains, biases, up_bias], [up],
        [((tokens, channels), BF), ((tokens, width), BF), ((tokens, width), F32)],
        [((channels, width), BF)], 13,
    )


def ff_down(place, second, act, biases, down):
    tokens, channels = second.shape

    def body(inputs, groups, outs, scratch):
        second, act, biases = inputs
        third = outs[0]
        (weight,) = scratch
        wait(groups[0][0])
        for at in range(0, channels, WIDE):
            cols = pl.ds(at, WIDE)
            total = second[:, cols].astype(F32) + dot(act[...], weight[:, cols])
            third[:, cols] = (total + biases[6:7, cols]).astype(BF)

    return run(
        body, place, [second, act, biases], [down], [((tokens, channels), BF)],
        [((act.shape[1], channels), BF)], 11,
    )[0]


def leave(place, third, frames, mask, biases, pair1):
    tokens, channels = third.shape

    def body(inputs, groups, outs, scratch):
        third, frames, mask, biases = inputs
        (weight,) = scratch
        wait(groups[0][0])
        for at in range(0, channels, WIDE):
            cols = pl.ds(at, WIDE)
            branch = dot(third[...], weight[:, cols]) + biases[4:5, cols]
            outs[0][:, cols] = (frames[:, cols].astype(F32) + mask[...] * branch).astype(BF)

    return run(
        body, place, [third, frames, mask, biases], [pair1], [((tokens, channels), BF)],
        [((channels, channels), BF)], 5,
    )[0]


def third_back(place, cotangent, mask, pair1):
    tokens, channels = cotangent.shape

    def body(inputs, groups, outs, scratch):
        cotangent, mask = inputs
        grad_branch, grad_third, sums = outs
        weight, acc = scratch
        acc[...] = jnp.zeros_like(acc)
        for at in range(0, tokens, STEP):
            rows = pl.ds(at, STEP)
            branch = (mask[rows, :] * cotangent[rows, :].astype(F32)).astype(BF)
            grad_branch[rows, :] = branch
            acc[...] += fold(branch.astype(F32))
        sums[0:1, :] = jnp.sum(acc[...], axis=0, keepdims=True)
        wait(groups[0][0])
        for at in range(0, channels, WIDE):
            cols = pl.ds(at, WIDE)
            third = dot_t(grad_branch[...], weight[cols, :]).astype(BF)
            grad_third[:, cols] = third
            sums[1:2, cols] = jnp.sum(fold(third.astype(F32)), axis=0, keepdims=True)

    square = ((tokens, channels), BF)
    return run(
        body, place, [cotangent, mask], [pair1], [square, square, ((2, channels), F32)],
        [((channels, channels), BF), ((8, channels), F32)], 5,
    )


def ff_back(place, grad_third, second, slope, gains, down, up):
    tokens, channels = second.shape
    width = slope.shape[1]

    def body(inputs, groups, outs, scratch):
        grad_third, second, slope, gains = inputs
        grad_up, grad_second, sums, up_sum = outs
        down_w, up_w, grad_in, acc = scratch
        acc[...] = jnp.zeros_like(acc)
        wait(groups[0][0])

        @pl.loop(0, width // WIDE)
        def _(i):
            cols = pl.ds(pl.multiple_of(i * WIDE, 128), WIDE)
            grad = (dot_t(grad_third[...], down_w[cols, :]) * slope[:, cols]).astype(BF)
            grad_up[:, cols] = grad
            up_sum[:, cols] = jnp.sum(fold(grad.astype(F32)), axis=0, keepdims=True)

        for copies in groups[1]:
            wait(copies)
        for at in range(0, channels, 256):
            cols = pl.ds(at, 256)
            grad_in[:, cols] = dot_t(grad_up[...], up_w[cols, :])
        for at in range(0, tokens, STEP):
            rows = pl.ds(at, STEP)
            hat, rstd = norm(second[rows, :].astype(F32))
            grad = grad_in[rows, :]
            third = grad_third[rows, :].astype(F32)
            total = (third + norm_back(grad * gains[2:3, :], hat, rstd)).astype(BF)
            grad_second[rows, :] = total
            acc[0:8, :] += fold(grad * hat)
            acc[8:16, :] += fold(grad)
            acc[16:24, :] += fold(total.astype(F32))
        for k in range(3):
            sums[k : k + 1, :] = jnp.sum(acc[8 * k : 8 * k + 8, :], axis=0, keepdims=True)

    square = ((tokens, channels), BF)
    return run(
        body, place, [grad_third, second, slope, gains], [down, up],
        [((tokens, width), BF), square, ((3, channels), F32), ((1, width), F32)],
        [
            ((width, channels), BF), ((channels, width), BF),
            ((tokens, channels), F32), ((24, channels), F32),
        ],
        18,
    )


def attend_back(place, grad_second, res, query, key, value, seqs, gains, attn, qkv):
    tokens, channels = res.shape
    dim = channels // HEADS
    scale = dim**-0.5

    def body(inputs, groups, outs, scratch):
        grad_second, res, query, key, value, seq_col, seq_row, clip_col, gains = inputs
        grad_q, grad_k, grad_v, grad_first, sums = outs
        attn_w, qkv_w, mixed, grad_in, acc = scratch[0], scratch[1:4], *scratch[4:]
        acc[...] = jnp.zeros_like(acc)
        wait(groups[0][0])
        for at in range(0, channels, WIDE):
            cols = pl.ds(at, WIDE)
            mixed[:, cols] = dot_t(grad_second[...], attn_w[cols, :]).astype(BF)
        for head in range(HEADS):
            cols = slice(head * dim, head * dim + dim)
            q, k, v, grad = query[:, cols], key[:, cols], value[:, cols], mixed[:, cols]
            probs = softmax(q, k, seq_col[...], seq_row[...], clip_col[...], scale)
            grad_probs = dot_t(grad, v)
            grad_v[:, cols] = dot_0(probs.astype(BF), grad).astype(BF)
            inner = jnp.sum(probs * grad_probs, axis=-1, keepdims=True)
            grad_scores = (probs * (grad_probs - inner)).astype(BF)
            grad_q[:, cols] = (dot(grad_scores, k) * scale).astype(BF)
            grad_k[:, cols] = (dot_0(grad_scores, q) * scale).astype(BF)
        for k in range(3):
            wait(groups[1 + k][0])
        for at in range(0, channels, 256):
            cols = pl.ds(at, 256)
            grad_in[:, cols] = (
                dot_t(grad_q[...], qkv_w[0][cols, :])
                + dot_t(grad_k[...], qkv_w[1][cols, :])
                + dot_t(grad_v[...], qkv_w[2][cols, :])
            )
        for at in range(0, tokens, STEP):
            rows = pl.ds(at, STEP)
            hat, rstd = norm(res[rows, :].astype(F32))
            grad = grad_in[rows, :]
            total = grad_second[rows, :].astype(F32) + norm_back(grad * gains[1:2, :], hat, rstd)
            total = total.astype(BF)
            grad_first[rows, :] = total
            acc[0:8, :] += fold(grad * hat)
            acc[8:16, :] += fold(grad)
            acc[16:24, :] += fold(total.astype(F32))
        for k in range(3):
            sums[k : k + 1, :] = jnp.sum(acc[8 * k : 8 * k + 8, :], axis=0, keepdims=True)

    square = ((tokens, channels), BF)
    return run(
        body, place, [grad_second, res, query, key, value, *seqs, gains], [attn, *qkv],
        [square] * 4 + [((3, channels), F32)],
        [((channels, channels), BF)] * 4
        + [square, ((tokens, channels), F32), ((24, channels), F32)],
        17,
    )


def enter_back(place, grad_frames, frames, cotangent, gains, pair0, pixels):
    tokens, channels = frames.shape

    def body(inputs, groups, outs, scratch):
        grad_frames, frames, cotangent, gains = inputs
        out, sums = outs
        weight, grad_hidden, acc = scratch
        acc[...] = jnp.zeros_like(acc)
        member = members(channels)
        stats = [group_stats(frames, unit, pixels, member) for unit in range(tokens // pixels)]
        wait(groups[0][0])
        for at in range(0, channels, WIDE):
            cols = pl.ds(at, WIDE)
            grad_hidden[:, cols] = dot_t(grad_frames[...], weight[cols, :])
        for chunks, mean, rstd, count in stats:
            plain, cross = 0.0, 0.0
            for rows in chunks:
                hat = (frames[rows, :].astype(F32) - mean) * rstd
                grad = grad_hidden[rows, :]
                acc[0:8, :] += fold(grad * hat)
                acc[8:16, :] += fold(grad)
                plain += fold(grad * gains[0:1, :])
                cross += fold(grad * gains[0:1, :] * hat)
            plain, cross = group_mean(plain, member, count), group_mean(cross, member, count)
            for rows in chunks:
                hat = (frames[rows, :].astype(F32) - mean) * rstd
                part = rstd * (grad_hidden[rows, :] * gains[0:1, :] - plain - hat * cross)
                out[rows, :] = (cotangent[rows, :].astype(F32) + part).astype(BF)
        for k in range(2):
            sums[k : k + 1, :] = jnp.sum(acc[8 * k : 8 * k + 8, :], axis=0, keepdims=True)

    return run(
        body, place, [grad_frames, frames, cotangent, gains], [pair0],
        [((tokens, channels), BF), ((2, channels), F32)],
        [((channels, channels), BF), ((tokens, channels), F32), ((16, channels), F32)],
        11,
    )


def pick(grid, value, axis, off, dim):
    size = grid.size(axis)
    part = value.shape[dim] // size
    place = (grid.at(axis) + off) % size
    return lax.dynamic_slice_in_dim(value, place * part, part, axis=dim)


def turn(place, grads, n1, n0):
    tokens = grads[0].shape[0]

    def kernel(place_ref, *refs):
        ins, outs, scratch = refs[: len(grads)], refs[len(grads) : -1], refs[-1]
        for g, ref in enumerate(ins):
            cols = ref.shape[1]
            share = cols // (n1 * n0)
            for at in range(0, cols, WIDE):
                piece = ref[:, at : at + WIDE].astype(F32).T
                scratch[at : at + WIDE, :] = piece.astype(BF)
            for off in range(n0):
                z0 = lax.rem(place_ref[3] + off, n0)
                for z1 in range(n1):
                    rows = pl.ds(pl.multiple_of((z1 * n0 + z0) * share, 16), share)
                    base = g * n1 * share + z1 * share
                    outs[off][base : base + share, :] = scratch[rows, :]

    vmem = pl.BlockSpec(memory_space=pltpu.VMEM)
    cols = sum(grad.shape[1] for grad in grads)
    shapes = [(cols // n0, tokens)] * n0
    return pl.pallas_call(
        kernel,
        out_shape=[jax.ShapeDtypeStruct(shape, BF) for shape in shapes],
        in_specs=[pl.BlockSpec(memory_space=pltpu.SMEM)] + [vmem] * len(grads),
        out_specs=[vmem] * len(shapes),
        scratch_shapes=[pltpu.VMEM((max(grad.shape[1] for grad in grads), tokens), BF)],
        compiler_params=pltpu.CompilerParams(vmem_limit_bytes=60 * 2**20),
        cost_estimate=pl.CostEstimate(flops=cols * 10**6, bytes_accessed=0, transcendentals=0),
    )(place, *grads)


def multiply(place, rights, lefts, groups, ny):
    rows, tokens = rights[0].shape
    cols = lefts[0].shape[1]
    block = rows // (groups * ny * CORES)
    mine = rows // CORES
    count = len(rights)

    def kernel(place_ref, *refs):
        rights, lefts, out, scratch = refs[:count], refs[count : 2 * count], refs[-2], refs[-1]
        for i, ref in enumerate(rights):
            for at in range(groups * ny):
                source = pl.ds(pl.multiple_of((at * CORES + place_ref[2]) * block, 16), block)
                scratch[at * block : (at + 1) * block, i * tokens : (i + 1) * tokens] = ref[source, :]
        high = mine // max(1, mine // 320)

        @pl.loop(0, cols // WIDE)
        def _(j):
            width = pl.ds(pl.multiple_of(j * WIDE, 128), WIDE)
            for at in range(0, mine, high):
                total = 0.0
                for i, ref in enumerate(lefts):
                    cells = scratch[at : at + high, i * tokens : (i + 1) * tokens]
                    total += dot(cells, ref[:, width])
                out[at : at + high, width] = total.astype(BF)

    vmem = pl.BlockSpec(memory_space=pltpu.VMEM)
    out = pl.pallas_call(
        kernel,
        out_shape=jax.ShapeDtypeStruct((mine, cols), BF),
        in_specs=[pl.BlockSpec(memory_space=pltpu.SMEM)] + [vmem] * (2 * count),
        out_specs=vmem,
        scratch_shapes=[pltpu.VMEM((mine, count * tokens), BF)],
        compiler_params=pltpu.CompilerParams(vmem_limit_bytes=60 * 2**20),
        cost_estimate=pl.CostEstimate(
            flops=2 * mine * cols * tokens * count, bytes_accessed=0, transcendentals=0
        ),
    )(place, *rights, *lefts)
    return out.reshape(groups, ny, block, cols)


class Hop:
    def __init__(self, grid, cells, axis, dim, *deps):
        self.mine = pick(grid, cells, axis, 0, dim)
        self.got = []
        for off in range(1, grid.size(axis)):
            send = pick(grid, cells, axis, off, dim)
            self.got.append(grid.shift(after(send, *deps) if deps else send, axis, off))

    def total(self, dtype=BF):
        return sum((got.astype(F32) for got in self.got), self.mine.astype(F32)).astype(dtype)


class Share:
    def __init__(self, grid, parts, axis):
        self.own = parts[0]
        self.got = [grid.shift(part, axis, off) for off, part in enumerate(parts[1:], 1)]

    def all(self):
        return [self.own] + self.got


def over_cores(grid, arrays):
    return arrays + [grid.shift(array, "c", 1) for array in arrays]


def tie(moves, *values):
    flat = [got for move in moves for got in move.got] + list(values)
    flat = list(lax.optimization_barrier(tuple(flat)))
    for move in moves:
        move.got, flat = flat[: len(move.got)], flat[len(move.got) :]
    return flat


def on_device(
    frames,
    cotangent,
    block_lengths,
    qkv_weight,
    pair_weight,
    attn_out_weight,
    ff_up_weight,
    ff_down_weight,
    norm_gains,
    biases,
    up_bias,
):
    micro_count, local_frames, pixels, channels = frames.shape[1:]
    grid = Grid(channels)
    block_count = block_lengths.shape[2]
    all_frames = block_count * CLIP
    pixel_share = pixels // grid.nf
    group = micro_count * pixel_share
    tokens = all_frames * group
    place = jnp.stack([grid.x, grid.y, grid.c, grid.z0]).astype(jnp.int32)
    n0, n1 = grid.n0, grid.size("z1")

    def to_pixels(rows):
        parts = rows.reshape(micro_count, local_frames, grid.nf, pixel_share, channels)
        parts = parts.transpose(2, 1, 0, 3, 4)
        parts = lax.all_to_all(parts, "frame", split_axis=0, concat_axis=0, tiled=True)
        return parts.reshape(tokens, channels)

    def to_frames(rows):
        parts = rows.reshape(grid.nf, local_frames, micro_count, pixel_share, channels)
        parts = lax.all_to_all(parts, "frame", split_axis=0, concat_axis=0, tiled=True)
        return parts.transpose(2, 1, 0, 3, 4).reshape(tokens, channels)

    clip_float = (block_lengths[0] > 1).astype(F32)
    frame_ids = lax.axis_index("frame") * local_frames + jnp.arange(local_frames, dtype=jnp.int32)
    block_pick = (
        frame_ids[:, None] // CLIP == jnp.arange(block_count, dtype=jnp.int32)[None, :]
    ).astype(F32)
    frame_mask = jnp.sum(clip_float[:, None, :] * block_pick[None], axis=-1)
    frame_mask = jnp.broadcast_to(
        frame_mask[:, :, None], (micro_count, local_frames, pixels)
    ).reshape(tokens, 1)
    token_mask = jnp.broadcast_to(
        clip_float.T[:, None, :, None], (block_count, CLIP, micro_count, pixel_share)
    ).reshape(tokens, 1)
    positions = jnp.broadcast_to(
        jnp.asarray(pos_table(channels))[None, :, None, :], (block_count, CLIP, group, channels)
    ).reshape(tokens, channels)
    ids = np.arange(tokens, dtype=np.int32)
    seq_ids = ids % group + ids // (group * CLIP) * group
    seqs = [jnp.asarray(seq_ids[:, None]), jnp.asarray(seq_ids[None, :]), token_mask]
    frames_flat = frames.reshape(tokens, channels)
    cotangent_flat = cotangent.reshape(tokens, channels)

    fold_by = ff_up_weight.shape[1] // channels
    squares = [qkv_weight[k] for k in range(3)] + [attn_out_weight, pair_weight[0], pair_weight[1]]
    cuts = [grid.cut(shard, 0, 1, "square") for shard in squares]
    up_cuts = [grid.cut(ff_up_weight, k, fold_by, "wide") for k in range(fold_by)]
    down_cuts = [grid.cut(ff_down_weight, k, fold_by, "tall") for k in range(fold_by)]
    half = fold_by // 2

    packet0 = Packet(grid, [cuts[4]])
    got0 = packet0.over_x()
    packet1 = Packet(grid, cuts[:1], *got0)
    got1 = packet1.over_x()
    packet0.over_y()
    packet2 = Packet(grid, cuts[1:3], *got1)
    got2 = packet2.over_x()
    pair0 = Weight(grid, pair_weight, 0, [(packet0, 0)], "square")
    hidden, first_res = enter(place, frames_flat, norm_gains, biases, pair0, pixels)
    packet1.over_y(packet0.mark, [first_res])
    res = to_pixels(first_res)
    packet3 = Packet(grid, [cuts[3]] + up_cuts[:half], first_res, *got1)
    got3 = packet3.over_x()
    packet2.over_y(packet1.mark, [first_res])
    packet4 = Packet(grid, up_cuts[half:] + [cuts[5]], *got2, *packet1.mark)
    got4 = packet4.over_x()
    qkv = [
        Weight(grid, qkv_weight, k, [(packet2, k - 1) if k else (packet1, 0)], "square")
        for k in range(3)
    ]
    inputs, query, key, value = project(place, res, norm_gains, biases, positions, qkv)
    grad_pixels = to_pixels(after(cotangent_flat, res))

    packet3.over_y(packet2.mark, [inputs])
    attn = Weight(grid, attn_out_weight[None], 0, [(packet3, 0)], "square")
    packet5 = Packet(grid, down_cuts[:half], inputs, *got3)
    got5 = packet5.over_x()
    mixed, second_res = attend(place, res, query, key, value, seqs, biases, attn)

    packet4.over_y(packet3.mark, [second_res])
    up = Weight(
        grid, ff_up_weight[None], 0,
        [(packet3, 1 + k) for k in range(half)] + [(packet4, k) for k in range(fold_by - half)],
        "wide",
    )
    pair1 = Weight(grid, pair_weight, 1, [(packet4, fold_by - half)], "square")
    packet6 = Packet(grid, down_cuts[half:], second_res, *got4)
    packet6.over_x()
    ff_in, act, slope = ff_up(place, second_res, norm_gains, biases, up_bias[None], up)
    inputs_z = Share(grid, [after(inputs, second_res)] * n0, "z0")
    mixed_z = Share(grid, [after(mixed, second_res)] * n0, "z0")
    ff_in, act = tie([inputs_z, mixed_z], ff_in, act)
    grad_branch, grad_third, sums_third = third_back(place, grad_pixels, token_mask, pair1)

    packet5.over_y(packet4.mark, [act])
    packet6.over_y(packet4.mark, [act])
    down = Weight(
        grid, ff_down_weight[None], 0,
        [(packet5, k) for k in range(half)] + [(packet6, k) for k in range(fold_by - half)], "tall",
    )
    ny, nz = grid.ny, n1 * n0
    rows_of = lambda arrays: over_cores(grid, arrays)
    (third_turned,) = turn(place, [grad_third], n1, 1)
    down_cells = multiply(place, rows_of([third_turned]), rows_of([act]), nz, ny)

    order = [z1 * n0 + z0 for z0 in range(n0) for z1 in range(n1)]
    stages = -(-nz // 4)
    parts = [order[k * stages : (k + 1) * stages] for k in range(-(-nz // stages))]

    def down_y(k):
        return [Hop(grid, down_cells[z], "y", 0) for z in parts[k]] if k < len(parts) else []

    def down_x(hops):
        return [Hop(grid, hop.total(), "x", 2) for hop in hops]

    ffin_z = Share(grid, [ff_in] * n0, "z0")
    down_a = down_y(0)
    grad_up, grad_second, sums_ff, up_sum = ff_back(
        place, after(grad_third, down_cells), second_res, slope, norm_gains, down, up
    )
    grad_up, grad_second, down_cells = tie(down_a + [ffin_z], grad_up, grad_second, down_cells)

    down_b, down_ax = down_y(1), down_x(down_a)
    ffin4, mixed4 = rows_of(ffin_z.all()), rows_of(mixed_z.all())
    up_turn, second_turn = turn(place, [grad_up], n1, n0), turn(place, [grad_second], n1, n0)
    up_z, second_z = Share(grid, up_turn, "z0"), Share(grid, second_turn, "z0")
    grad_query, grad_key, grad_value, grad_first, sums_attn = attend_back(
        place, after(grad_second, *up_turn), res, query, key, value, seqs, norm_gains, attn, qkv
    )
    grad_query, grad_key, grad_value, grad_first, down_cells = tie(
        down_b + down_ax + [up_z, second_z], grad_query, grad_key, grad_value, grad_first, down_cells
    )

    grad_frames = to_frames(grad_first)
    down_c, down_bx = down_y(2), down_x(down_b)
    qkv_z = Share(grid, turn(place, [grad_query, grad_key, grad_value], n1, n0), "z0")
    up_cells = multiply(place, rows_of(up_z.all()), ffin4, n1, ny)
    second_cells = multiply(place, rows_of(second_z.all()), mixed4, n1, ny)
    third_res = ff_down(place, after(second_res, grad_first), act, biases, down)
    grad_frames, third_res, up_cells, second_cells, down_cells = tie(
        down_c + down_bx + [qkv_z], grad_frames, third_res, up_cells, second_cells, down_cells
    )

    down_d, down_cx = down_y(3), down_x(down_c)
    up_x = [Hop(grid, up_cells[z], "x", 2) for z in range(n1)]
    frames_grad, sums_enter = enter_back(
        place, grad_frames, frames_flat, cotangent_flat, norm_gains, pair0, pixels
    )
    qkv_right, inputs4 = rows_of(qkv_z.all()), rows_of(inputs_z.all())
    (last_turn,) = turn(place, [grad_frames], n1, 1)
    (branch_turn,) = turn(place, [grad_branch], n1, 1)
    last_right, last_left = rows_of([last_turn]), rows_of([hidden])
    branch_right, branch_left = rows_of([branch_turn]), rows_of([third_res])
    qkv_cells = multiply(place, qkv_right, inputs4, 3 * n1, ny)
    last_cells = multiply(place, last_right, last_left, nz, ny)
    branch_cells = multiply(place, branch_right, branch_left, nz, ny)
    qkv_cells, last_cells, branch_cells, third_res, frames_grad, sums_enter = tie(
        down_d + down_cx + up_x[:1],
        qkv_cells, last_cells, branch_cells, third_res, frames_grad, sums_enter,
    )

    down_dx = down_x(down_d)
    second_y = Hop(grid, second_cells, "y", 1)
    last_y = Hop(grid, last_cells, "y", 1)
    up_y = [Hop(grid, up_x[0].total(), "y", 0)]
    third_frames = to_frames(third_res)
    (qkv_cells,) = tie(down_dx + up_x[1:] + [second_y, last_y] + up_y, qkv_cells)

    qkv_x = Hop(grid, qkv_cells, "x", 3)
    up_y += [Hop(grid, hop.total(), "y", 0) for hop in up_x[1:]]
    down_parts = down_ax + down_bx + down_cx + down_dx
    down_whole = [None] * nz
    for z, hop in zip([z for part in parts for z in part], down_parts):
        down_whole[z] = hop.total()
    down_whole = jnp.stack(down_whole).reshape(n1, n0, *down_whole[0].shape[1:])
    down_z1 = Hop(grid, down_whole, "z1", 0)
    totals = [sums_third, sums_ff, sums_attn, up_sum.reshape(-1, channels), sums_enter]
    totals = grid.total(jnp.concatenate(totals, axis=0))
    (branch_cells, third_frames, totals) = tie(
        [qkv_x, down_z1] + up_y[1:], branch_cells, third_frames, totals
    )

    result = leave(place, third_frames, frames_flat, frame_mask, biases, pair1)
    branch_x = Hop(grid, branch_cells, "x", 3)
    second_x, last_x = Hop(grid, second_y.total(), "x", 3), Hop(grid, last_y.total(), "x", 3)
    qkv_y = Hop(grid, qkv_x.total(), "y", 1)
    up_whole = jnp.stack([hop.total() for hop in up_y])
    up_z1 = Hop(grid, up_whole, "z1", 0)
    down_z0 = Hop(grid, down_z1.total(), "z0", 1)
    (result,) = tie([branch_x, second_x, last_x, qkv_y, up_z1, down_z0], result)

    branch_y = Hop(grid, branch_x.total(), "y", 1)
    block = channels // grid.nf
    squares = [second_x.total().reshape(1, n1, block, -1), qkv_y.total().reshape(3, n1, block, -1)]
    squares_z1 = Hop(grid, jnp.concatenate(squares, axis=0), "z1", 1)
    last_z1 = Hop(grid, last_x.total().reshape(n1, n0, block, -1), "z1", 0)
    tie([branch_y, squares_z1, last_z1])
    branch_z1 = Hop(grid, branch_y.total().reshape(n1, n0, block, -1), "z1", 0)
    last_z0 = Hop(grid, last_z1.total(), "z0", 1)
    tie([branch_z1, last_z0])
    branch_z0 = Hop(grid, branch_z1.total(), "z0", 1)

    def own(hop, count=1):
        total = hop.total(F32)
        return total.reshape(count, -1, total.shape[-1]).transpose(0, 2, 1)

    squares_own = own(squares_z1, 4)
    attn_own, qkv_own = squares_own[0], squares_own[1:]
    up_own, down_own = own(up_z1)[0], own(down_z0)[0]
    pair_own = jnp.concatenate([own(last_z0), own(branch_z0)], axis=0)
    gain_sum = jnp.stack([totals[-2], totals[5], totals[2]])
    bias_sum = jnp.stack([totals[-1]] + [totals[k] for k in (6, 7, 4, 0, 3, 1)])
    upb_sum = totals[8:-2].reshape(-1)
    return (
        result.reshape(frames.shape),
        frames_grad.reshape(frames.shape),
        qkv_own,
        pair_own,
        attn_own,
        up_own,
        down_own,
        gain_sum,
        bias_sum,
        upb_sum,
    )


def solution(mesh):
    placed = (
        P("fsdp", None, "frame", None, None),
        P("fsdp", None, "frame", None, None),
        P("fsdp", None, None),
        P(None, "fsdp", None),
        P(None, "fsdp", None),
        P("fsdp", None),
        P("fsdp", None),
        P("fsdp", None),
        P(),
        P(),
        P(),
    )
    return jax.shard_map(
        on_device,
        mesh=mesh,
        in_specs=placed,
        out_specs=(
            P("fsdp", None, "frame", None, None),
            P("fsdp", None, "frame", None, None),
            P(None, "fsdp", "frame"),
            P(None, "fsdp", "frame"),
            P("fsdp", "frame"),
            P("fsdp", "frame"),
            P("fsdp", "frame"),
            P(),
            P(),
            P(),
        ),
        check_vma=False,
    )
```
